1024 devices in a mesh: dp: 32 (over z_hi, y, core), seq: 32 (over z_lo, x).
Axes of the slice: x: 4, y: 4, z: 32 (z_hi: 4, z_lo: 8; z = z_hi * 8 + z_lo), core: 2. Of those that a mesh axis runs over, the one named last changes fastest.
Arguments:
- queries: bfloat16 [32, 4096, 4096], P('dp', 'seq'), may hold values from -150 to 150
- keys: bfloat16 [32, 4096, 512], P('dp', 'seq'), may hold values from -6 to 6
- values: bfloat16 [32, 4096, 512], P('dp', 'seq'), may hold values from -6 to 6
- grad_out: bfloat16 [32, 4096, 4096], P('dp', 'seq'), may hold values from -6 to 6
- proj_in: bfloat16 [32, 4096, 256], P('dp', 'seq'), may hold values from -6 to 6
- segments: int32 [32, 4096], P('dp'), may hold values from 0 to 63, never falling along the last dimension, each value on 1 to 128 neighbouring positions
Outputs:
- grad_q_proj: float32 [256, 4096], P('dp', 'seq')
- grad_kv_proj: float32 [256, 1024], P('dp', 'seq')
The draws below stay inside these ranges and needn't reach their ends.
Inputs may be any that keep to these rules, and one draw needn't show every extreme that they name: `segments`: document numbers never fall along a sequence; each document has 1 to 128 tokens, and some document has exactly 128.
All inputs are finite; a program needn't handle non-finite values.
Results may differ from the reference program's by a relative error of at most 0.025.
Values may be sent and summed in bfloat16 or wider, within the bound.
A program may use at most 64 MiB of HBM per device.

```python
import math
import jax
import jax.numpy as jnp
import numpy as np
from jax import lax

H = 32
KV = 4
HD = 128
RANK = 256
DOC = 128
SEQ_LEN = 4096
SEQS = 32


def paired_draw(key):
    base = jax.random.fold_in(key, 7)
    key_q, key_k = jax.random.split(base, 2)
    queries = jnp.clip(jax.random.normal(key_q, (SEQS, SEQ_LEN, H * HD), jnp.float32), -6.0, 6.0)
    keys = jnp.clip(jax.random.normal(key_k, (SEQS, SEQ_LEN, KV * HD), jnp.float32), -6.0, 6.0)
    return (queries, keys)


def draw_queries(key, part):
    return paired_draw(key)[0].astype(jnp.bfloat16)


def draw_keys(key, part):
    return paired_draw(key)[1].astype(jnp.bfloat16)


def strengthened(values, rng, source, target, shards_of, factor):
    def block_of(axis_at):
        return (jnp.arange(values.shape[axis_at]) // (values.shape[axis_at] // shards_of)).reshape((-1,) + (1,) * (values.ndim - 1 - axis_at))

    one_side = jax.random.permutation(rng, shards_of)[block_of(target)]
    other_side = (block_of(target) + shards_of // 2) % shards_of
    return jnp.where((block_of(source) == one_side) | (block_of(source) == other_side), factor * values, values)


def steps_of(stream_key, shape, pieces, low, top_value):
    loudness = 1.0
    for position, blocks in pieces:
        steps = jax.random.uniform(jax.random.fold_in(jax.random.fold_in(stream_key, 6), position), (blocks,), jnp.float32, low / len(pieces), top_value / len(pieces))
        loudness = loudness * jnp.repeat(jnp.exp(steps), shape[position] // blocks).reshape((-1,) + (1,) * (len(shape) - 1 - position))
    return loudness


def split_up(count, total, bound, lean):
    loads = [(1 << 20) // math.isqrt(rank ** lean) + 1 for rank in range(2, count + 1)]
    spare, given = total - bound - (count - 1), [1] * (count - 1)
    while spare > 0:
        movable = [i for i in range(count - 1) if given[i] < bound]
        pool, left = sum([loads[i] for i in movable]), spare
        for i in movable:
            more = min(bound - given[i], max(1, left * loads[i] // pool), spare)
            given[i] = given[i] + more
            spare = spare - more
    return np.array([bound] + given)


def uneven(rng, amount, total, bound, skew):
    if amount == 2:
        one = jax.random.randint(rng, (), max(1, total - bound), min(bound, total - 1) + 1)
        return jnp.stack([one, total - one])
    sizes = jnp.asarray(split_up(amount, total, bound, skew), jnp.int32)
    pairs = (amount - 1) // 2
    source_of, taker = sizes[1:1 + 2 * pairs:2], sizes[2:2 + 2 * pairs:2]
    margin = jnp.minimum(source_of - 1, bound - taker)
    passed = jax.random.randint(jax.random.fold_in(rng, 1), (pairs,), 0, 1 << 20) % (margin + 1)
    sizes = sizes.at[1:1 + 2 * pairs:2].set(source_of - passed).at[2:2 + 2 * pairs:2].set(taker + passed)
    return sizes[jax.random.permutation(jax.random.fold_in(rng, 2), amount)]


def gaussian(own_key, shape, deviation, most, cuts=(), held_as=jnp.bfloat16):
    level = steps_of(own_key, shape, cuts, -0.22, 0.18) if cuts else 1.0
    result = jax.random.normal(own_key, shape, jnp.float32) * deviation * level
    return jnp.minimum(jnp.maximum(result, -most), most).astype(held_as)


def noise_with(key, shape, scale, limit, cuts, heavy, dtype=jnp.bfloat16):
    result = scale * jax.random.normal(key, shape, jnp.float32)
    if cuts:
        result = result * steps_of(key, shape, cuts, -0.22, 0.18)
    return jnp.clip(strengthened(result, jax.random.fold_in(key, 3), *heavy), -limit, limit).astype(dtype)


def setup_inputs(seed: int = 0) -> dict:
    seeds = jax.random.split(jax.random.key(seed), 7)
    queries = draw_queries(jax.random.fold_in(seeds[6], 71), 0)
    keys = draw_keys(jax.random.fold_in(seeds[6], 71), 0)
    values = gaussian(seeds[2], (SEQS, SEQ_LEN, KV * HD), 1.0, 6.0, ((0, 32), (1, 32)))
    grad_out = gaussian(seeds[3], (SEQS, SEQ_LEN, H * HD), 1.0, 6.0, ((0, 32), (1, 32)))
    proj_in = noise_with(seeds[4], (SEQS, SEQ_LEN, RANK), 1.0, 6.0, ((0, 32), (1, 32)), (0, 2, 32, 2.75))
    segments = jax.vmap(lambda own: jnp.searchsorted(jnp.cumsum(uneven(own, 2 * SEQ_LEN // DOC, SEQ_LEN, DOC, 1)), jnp.arange(SEQ_LEN), side="right"))(jax.random.split(seeds[5], SEQS)).reshape((SEQS, SEQ_LEN)).astype(jnp.int32)
    return {"queries": queries, "keys": keys, "values": values, "grad_out": grad_out, "proj_in": proj_in, "segments": segments}


def shifted_window(blocks, filler):
    previous = jnp.concatenate([jnp.full_like(blocks[:1], filler), blocks[:-1]], axis=0)
    return jnp.concatenate([previous, blocks], axis=1)


def attend(q_heads, k_heads, v_heads, g_heads, segment):
    length = q_heads.shape[0]
    head_count = q_heads.shape[1]
    head_width = q_heads.shape[2]
    block_count = length // DOC
    group_size = min(512 // DOC, block_count)
    scaling = head_width ** -0.5

    def to_blocks(array):
        return array.reshape((block_count, DOC) + array.shape[1:])

    def grouped(array):
        return array.reshape((block_count // group_size, group_size) + array.shape[1:])

    seg_query = to_blocks(segment)
    seg_key = shifted_window(seg_query, -1)
    q_block = to_blocks(q_heads)
    g_block = to_blocks(g_heads)
    k_window = shifted_window(to_blocks(k_heads), 0.0)
    v_window = shifted_window(to_blocks(v_heads), 0.0)
    causal = jnp.arange(2 * DOC)[None, :] <= jnp.arange(DOC)[:, None] + DOC

    def one_group(items):
        q_part, g_part, k_part, v_part, sq_part, sk_part = items
        q_part = q_part.astype(jnp.float32)
        g_part = g_part.astype(jnp.float32)
        k_part = k_part.astype(jnp.float32)
        v_part = v_part.astype(jnp.float32)
        allowed = (sq_part[:, :, None] == sk_part[:, None, :]) & causal[None]
        allowed = allowed[:, None]
        scores = jnp.einsum('nqhd,nkhd->nhqk', q_part, k_part) * scaling
        scores = jnp.where(allowed, scores, -1e30)
        probs = jnp.exp(scores - jnp.max(scores, axis=-1, keepdims=True))
        probs = jnp.where(allowed, probs, 0.0)
        probs = probs / jnp.sum(probs, axis=-1, keepdims=True)
        probs_b = probs.astype(jnp.bfloat16)
        attn_out = jnp.einsum('nhqk,nkhd->nqhd', probs_b.astype(jnp.float32), v_part).astype(jnp.bfloat16)
        delta = jnp.sum(g_part * attn_out.astype(jnp.float32), axis=-1)
        dprobs = jnp.einsum('nqhd,nkhd->nhqk', g_part, v_part)
        dscore = (probs * (dprobs - jnp.transpose(delta, (0, 2, 1))[..., None]) * scaling).astype(jnp.bfloat16)
        dq_part = jnp.einsum('nhqk,nkhd->nqhd', dscore.astype(jnp.float32), k_part).astype(jnp.bfloat16)
        dk_part = jnp.einsum('nhqk,nqhd->nkhd', dscore.astype(jnp.float32), q_part)
        dv_part = jnp.einsum('nhqk,nqhd->nkhd', probs_b.astype(jnp.float32), g_part)
        return dq_part, dk_part, dv_part

    items = tuple(grouped(array) for array in (q_block, g_block, k_window, v_window, seg_query, seg_key))
    dq_all, dk_window, dv_window = lax.map(one_group, items)
    dq_all = dq_all.reshape(length, head_count, head_width)

    def fold_window(window):
        window = window.reshape((block_count, 2 * DOC, head_count, head_width))
        later = jnp.concatenate([window[1:, :DOC], jnp.zeros_like(window[:1, :DOC])], axis=0)
        return (window[:, DOC:] + later).reshape(length, head_count, head_width).astype(jnp.bfloat16)

    return dq_all, fold_window(dk_window), fold_window(dv_window)


def reference(queries, keys, values, grad_out, proj_in, segments):
    per_group = H // KV

    def one_sequence(carry, items):
        q_seq, k_seq, v_seq, g_seq, rows, segment = items
        q_heads = q_seq.reshape(SEQ_LEN, H, HD)
        k_heads = jnp.repeat(k_seq.reshape(SEQ_LEN, KV, HD), per_group, axis=1)
        v_heads = jnp.repeat(v_seq.reshape(SEQ_LEN, KV, HD), per_group, axis=1)
        g_heads = g_seq.reshape(SEQ_LEN, H, HD)
        dq_all, dk_all, dv_all = attend(q_heads, k_heads, v_heads, g_heads, segment)
        rows_f = rows.astype(jnp.float32)
        q_term = jnp.einsum('lr,lhd->rhd', rows_f, dq_all.astype(jnp.float32)).reshape(RANK, H * HD)
        k_term = jnp.einsum('lr,lhd->rhd', rows_f, dk_all.astype(jnp.float32)).reshape(RANK, KV, per_group, HD).sum(axis=2)
        v_term = jnp.einsum('lr,lhd->rhd', rows_f, dv_all.astype(jnp.float32)).reshape(RANK, KV, per_group, HD).sum(axis=2)
        kv_term = jnp.stack([k_term, v_term], axis=1).reshape(RANK, 2 * KV * HD)
        return (carry[0] + q_term, carry[1] + kv_term), None

    start = (jnp.zeros((RANK, H * HD), jnp.float32), jnp.zeros((RANK, 2 * KV * HD), jnp.float32))
    (grad_q_proj, grad_kv_proj), unused = lax.scan(one_sequence, start, (queries, keys, values, grad_out, proj_in, segments))
    return grad_q_proj, grad_kv_proj
```

```python
import functools
import math

import jax
import jax.numpy as jnp
from jax import lax
from jax.experimental import pallas as pl
from jax.experimental.pallas import tpu as pltpu
from jax.sharding import PartitionSpec as P

MESH = pl.DeviceIdType.MESH
F32 = jnp.float32
BF16 = jnp.bfloat16
B = 128
NEG = -1e30


def nt(a, b):
    return lax.dot_general(a, b, (((1,), (1,)), ((), ())), preferred_element_type=F32)


def tn(a, b):
    return lax.dot_general(a, b, (((0,), (0,)), ((), ())), preferred_element_type=F32)


def nn(a, b):
    return lax.dot_general(a, b, (((1,), (0,)), ((), ())), preferred_element_type=F32)


class Grid:
    def __init__(self, ZH, Y, C, ZL, X):
        self.ZH, self.Y, self.C, self.ZL, self.X = ZH, Y, C, ZL, X
        self.Z = ZH * ZL
        self.G = ZL // 2


REAL = Grid(4, 4, 2, 8, 4)


def kernel(
    gr,
    q_hbm, k_hbm, v_hbm, do_hbm, pj_hbm, seg_hbm,
    out_ref,
    seg_ref,     q_v, do_v, kvw, pjw, pjt, bias, mo, mp, pw, dsw,
    own, csend, crecv, s1, r1, s2, r2, zq, zkv, zsrc, zr,
    ld_sem, kv_sem, pj_sem, sg_sem, hs_sem, hr_sem, cs_sem, cr_sem, s1s_sem, s1r_sem, s2s_sem, s2r_sem, zs_sem, zr_sem, rel_sem,
):
    ZH, Y, ZL, X, Z, G = gr.ZH, gr.Y, gr.ZL, gr.X, gr.Z, gr.G
    HG = 2 * X
    SEQ = ZL * X
    dp, seq = lax.axis_index("dp"), lax.axis_index("seq")
    zh, y, c = dp // (2 * Y), (dp // 2) % Y, dp % 2
    zl, x = seq // X, seq % X
    z = zh * ZL + zl

    def at(zh_, y_, c_, zl_, x_):
        return ((zh_ * Y + y_) * 2 + c_, zl_ * X + x_)

    def along_z(k):
        there = lax.rem(z + k + Z, Z)
        return at(there // ZL, y, c, lax.rem(there, ZL), x)

    def along_y(k):
        return at(zh, lax.rem(y + k, Y), c, zl, x)

    def along_x(k):
        return at(zh, y, c, zl, lax.rem(x + k, X))

    other = at(zh, y, 1 - c, zl, x)
    right = (dp, jnp.minimum(seq + 1, SEQ - 1))
    left = (dp, jnp.maximum(seq - 1, 0))

    def local(src, dst, sem):
        copy = pltpu.make_async_copy(src, dst, sem)
        copy.start()
        return copy

    def remote(src, dst, ssem, rsem, device):
        return pltpu.make_async_remote_copy(src, dst, ssem, rsem, device_id=device, device_id_type=MESH)

    def await_bytes(ref, sem):
        pltpu.make_async_copy(ref, ref, sem).wait()

    seg_in = local(seg_hbm, seg_ref, sg_sem)
    kv_in = []
    for g in range(G):
        cols = pl.ds(g * B, B)
        kv_in.append(local(k_hbm.at[0, :, cols], kvw.at[g, 0, pl.ds(0, B)], kv_sem.at[g, 0]))
        kv_in.append(local(v_hbm.at[0, :, cols], kvw.at[g, 1, pl.ds(0, B)], kv_sem.at[g, 1]))
    pj_in = local(pj_hbm.at[0], pjw.at[0], pj_sem)
    big = []
    for g in range(G):
        cols = pl.ds(g * HG * B, HG * B)
        big.append(
            (
                local(q_hbm.at[0, :, cols], q_v.at[:, cols], ld_sem.at[g, 0]),
                local(do_hbm.at[0, :, cols], do_v.at[:, cols], ld_sem.at[g, 1]),
            )
        )

    barrier = pltpu.get_barrier_semaphore()
    near = [other]
    near += [along_y(k) for k in range(1, Y)]
    near += [along_x(k) for k in range(1, X)]
    near += [along_z(k) for k in (1, -1, 2, -2)]
    for device in near:
        pl.semaphore_signal(barrier, inc=1, device_id=device, device_id_type=MESH)

    @pl.when(seq > 0)
    def _():
        pl.semaphore_signal(barrier, inc=1, device_id=left, device_id_type=MESH)

    seg_in.wait()
    start = pl.multiple_of(seq * B, B)
    start_before = pl.multiple_of(jnp.maximum(seq - 1, 0) * B, B)
    seg_i = jnp.broadcast_to(seg_ref[:, pl.ds(start, B)].astype(F32), (B, B))
    seg_p = jnp.broadcast_to(seg_ref[:, pl.ds(start_before, B)].astype(F32), (B, B))
    seg_p = jnp.where(seq > 0, seg_p, -1.0)
    row = lax.broadcasted_iota(jnp.int32, (B, B), 0)
    lane = lax.broadcasted_iota(jnp.int32, (B, B), 1)
    causal = row <= lane
    same = jnp.where(causal, seg_i.T, seg_p.T) == seg_i
    one_bias = jnp.where(same, 0.0, NEG)
    one_mo = jnp.where(causal, 1.0, 0.0).astype(BF16)
    one_mp = jnp.where(causal, 0.0, 1.0).astype(BF16)
    for half in range(2):
        cols = pl.ds(half * B, B)
        bias[:, cols] = one_bias
        mo[:, cols] = one_mo
        mp[:, cols] = one_mp

    for copy in kv_in:
        copy.wait()
    pj_in.wait()

    @pl.when(seq < SEQ - 1)
    def _():
        pl.semaphore_wait(barrier, len(near) + 1)

    @pl.when(seq == SEQ - 1)
    def _():
        pl.semaphore_wait(barrier, len(near))

    def halo_kv(g):
        return remote(
            kvw.at[g, :, pl.ds(0, B)], kvw.at[g, :, pl.ds(B, B)], hs_sem.at[g], hr_sem.at[g], right
        )

    halo_pj = remote(pjw.at[0], pjw.at[1], hs_sem.at[G], hr_sem.at[G], right)

    @pl.when(seq < SEQ - 1)
    def _():
        halo_kv(0).start()
        halo_pj.start()
        for g in range(1, G):
            halo_kv(g).start()

    @pl.when(seq == 0)
    def _():
        kvw[:, :, B:] = jnp.zeros((G, 2, B, B), BF16)
        pjw[1] = jnp.zeros(pjw.shape[1:], BF16)

    relays = []
    reach = 2
    while reach < Z // 2:
        relays.append(reach)
        reach *= 2

    def relay_out(n):
        for k in (relays[n], -relays[n]):
            pl.semaphore_signal(rel_sem.at[n], inc=1, device_id=along_z(k), device_id_type=MESH)

    def relay_in(n):
        pl.semaphore_wait(rel_sem.at[n], 2)

    relay_out(0)

    first_core = c == 0

    def transposed(n):
        t = pjw[n].astype(F32).T
        mine, theirs = [], []
        for yy in range(Y):
            for hh in range(ZH):
                o = (hh * Y + yy) * 2
                even, odd = t[o * 8 : o * 8 + 8], t[o * 8 + 8 : o * 8 + 16]
                mine.append(jnp.where(first_core, even, odd))
                theirs.append(jnp.where(first_core, odd, even))
        pjt[:, n * B : (n + 1) * B] = jnp.concatenate(mine + theirs, axis=0).astype(BF16)

    transposed(0)
    R = pjt.shape[0] // 2
    YR = R // Y

    scale = B**-0.5
    to_log2 = scale * math.log2(math.e)
    row2 = lax.broadcasted_iota(jnp.int32, (B, 2 * B), 0)
    lane2 = lax.broadcasted_iota(jnp.int32, (B, 2 * B), 1)
    causal2 = row2 <= jnp.bitwise_and(lane2, B - 1)

    def stacked(ref, off, count):
        return jnp.concatenate([ref[:, off + n * B : off + (n + 1) * B] for n in range(count)], axis=0)

    def compute(g):
        base = g * HG * B
        for copy in big[g]:
            copy.wait()

        @pl.when(seq > 0)
        def _():
            halo_kv(g).wait_recv()

        kw, vw = kvw[g, 0], kvw[g, 1]
        for hp in range(HG // 2):
            off = base + hp * 2 * B
            st = nt(kw, stacked(q_v, off, 2))
            dpt = nt(vw, stacked(do_v, off, 2))
            s = jnp.where(causal2, st[:B], st[B:]) * to_log2 + bias[...]
            p = jnp.exp2(s - jnp.max(s, axis=0, keepdims=True))
            p = p * (1.0 / jnp.sum(p, axis=0, keepdims=True))
            d = jnp.where(causal2, dpt[:B], dpt[B:])
            delta = jnp.sum(p * d, axis=0, keepdims=True)
            ds = (p * ((d - delta) * scale)).astype(BF16)
            pb = p.astype(BF16)
            cols = pl.ds(hp * 2 * B, 2 * B)
            pw[:B, cols] = pb * mo[...]
            pw[B:, cols] = pb * mp[...]
            dsw[:B, cols] = ds * mo[...]
            dsw[B:, cols] = ds * mp[...]
        if g == 0:

            @pl.when(seq > 0)
            def _():
                halo_pj.wait_recv()

            transposed(1)
        dqt = tn(kw, dsw[...]).astype(BF16)
        dk = nn(dsw[...], stacked(q_v, base, HG))
        dv = nn(pw[...], stacked(do_v, base, HG))
        for hp in range(HG // 2):
            lo = hp * 2 * B
            pair = jnp.concatenate([dqt[:, lo : lo + B], dqt[:, lo + B : lo + 2 * B]], axis=0)
            gq = nt(pjt[:, :B], pair)
            for n in range(2):
                own[g, 2 * hp + n] = gq[:R, n * B : (n + 1) * B]
                csend[g, 2 * hp + n] = gq[R:, n * B : (n + 1) * B].astype(BF16)
        gkv = nn(pjt[...], jnp.concatenate([dk, dv], axis=1).astype(BF16))
        for n in range(2):
            own[g, HG + n] = gkv[:R, n * B : (n + 1) * B]
            csend[g, HG + n] = gkv[R:, n * B : (n + 1) * B].astype(BF16)

    def core_copy(g):
        return remote(csend.at[g], crecv.at[g], cs_sem.at[g], cr_sem.at[g], other)

    def s1_copy(g, k):
        rows = pl.ds(pl.multiple_of(lax.rem(y + k, Y) * YR, YR), YR)
        return remote(s1.at[g, :, rows], r1.at[g, k - 1], s1s_sem.at[g], s1r_sem.at[g], along_y(k))

    def s2_copy(g, k):
        return remote(s2.at[g, lax.rem(x + k, X)], r2.at[g, k - 1], s2s_sem.at[g], s2r_sem.at[g], along_x(k))

    def step1(g):
        core_copy(g).wait_recv()
        s1[g] = (own[g] + crecv[g].astype(F32)).astype(BF16)
        for k in range(1, Y):
            s1_copy(g, k).start()

    def step2(g):
        await_bytes(r1.at[g], s1r_sem.at[g])
        rows = pl.ds(pl.multiple_of(y * YR, YR), YR)
        total = s1[g, :, rows].astype(F32)
        for k in range(1, Y):
            total = total + r1[g, k - 1].astype(F32)
        total = total.astype(BF16)
        for xx in range(X):
            s2[g, xx, 0] = total[xx]
            s2[g, xx, 1] = total[X + xx]
            s2[g, xx, 2] = total[HG]
            s2[g, xx, 3] = total[HG + 1]
        for k in range(1, X):
            s2_copy(g, k).start()

    def step3(g):
        await_bytes(r2.at[g], s2r_sem.at[g])
        total = s2[g, x].astype(F32)
        for k in range(1, X):
            total = total + r2[g, k - 1].astype(F32)
        zq[2 * g] = total[0]
        zq[2 * g + 1] = total[1]
        zkv[g] = total[2]
        zkv[G + g] = total[3]

    sent = set()

    def z_send(done):
        ready = [n for n in range(ZL) if n // 2 < done and n % G < done and n not in sent]
        sent.update(ready)
        for n in ready:
            for hh in range(ZH):
                rows = pl.ds(hh * 8, 8)
                zsrc[n, hh] = jnp.concatenate([zq[n, rows], zkv[n, rows]], axis=0).astype(BF16)
        for j in sorted(range(ZH), key=lambda j: -min(j, ZH - j)):
            for n in ready:
                zh_to = lax.rem(zh + j, ZH)
                k = lax.rem(zh_to * ZL + n - z + Z, Z)

                @pl.when(k != 0)
                def _():
                    remote(
                        zsrc.at[n, zh_to], zr.at[k - 1], zs_sem, zr_sem, at(zh_to, y, c, n, x)
                    ).start()

    for g in range(G):
        compute(g)
        core_copy(g).start()
        if g < len(relays):
            relay_in(g)
            if g + 1 < len(relays):
                relay_out(g + 1)
        if g >= 1:
            step1(g - 1)
        if g >= 2:
            step2(g - 2)
        if g >= 3:
            step3(g - 3)
    step1(G - 1)
    if G >= 2:
        step2(G - 2)
    if G >= 3:
        step3(G - 3)
        z_send(G - 2)
    if G >= 2:
        step3(G - 2)
        z_send(G - 1)
    step2(G - 1)
    step3(G - 1)
    z_send(G)

    @pl.when(seq < SEQ - 1)
    def _():
        for g in range(G):
            halo_kv(g).wait_send()
        halo_pj.wait_send()

    for g in range(G):
        core_copy(g).wait_send()
        await_bytes(r1.at[g], s1s_sem.at[g])
        await_bytes(r2.at[g], s2s_sem.at[g])
    await_bytes(zr, zs_sem)
    await_bytes(zr, zr_sem)
    total = zsrc[zl, zh].astype(F32)
    for k in range(Z - 1):
        total = total + zr[k].astype(F32)
    out_ref[...] = total


def on_device(gr, queries, keys, values, grad_out, proj_in, segments):
    G, X, Y, ZH, ZL, Z = gr.G, gr.X, gr.Y, gr.ZH, gr.ZL, gr.Z
    HG = 2 * X
    NB = HG + 2
    rank = proj_in.shape[-1]
    R = rank // 2
    YR = R // Y
    hbm = pl.BlockSpec(memory_space=pltpu.HBM)
    vmem = pl.BlockSpec(memory_space=pltpu.VMEM)
    dma = pltpu.SemaphoreType.DMA
    out = pl.pallas_call(
        functools.partial(kernel, gr),
        out_shape=jax.ShapeDtypeStruct((16, B), F32),
        in_specs=[hbm] * 6,
        out_specs=vmem,
        scratch_shapes=[
            pltpu.VMEM(segments.shape, jnp.int32),
            pltpu.VMEM((B, G * HG * B), BF16),
            pltpu.VMEM((B, G * HG * B), BF16),
            pltpu.VMEM((G, 2, 2 * B, B), BF16),
            pltpu.VMEM((2, B, rank), BF16),
            pltpu.VMEM((rank, 2 * B), BF16),
            pltpu.VMEM((B, 2 * B), F32),
            pltpu.VMEM((B, 2 * B), BF16),
            pltpu.VMEM((B, 2 * B), BF16),
            pltpu.VMEM((2 * B, HG * B), BF16),
            pltpu.VMEM((2 * B, HG * B), BF16),
            pltpu.VMEM((G, NB, R, B), F32),
            pltpu.VMEM((G, NB, R, B), BF16),
            pltpu.VMEM((G, NB, R, B), BF16),
            pltpu.VMEM((G, NB, R, B), BF16),
            pltpu.VMEM((G, Y - 1, NB, YR, B), BF16),
            pltpu.VMEM((G, X, 4, YR, B), BF16),
            pltpu.VMEM((G, X - 1, 4, YR, B), BF16),
            pltpu.VMEM((ZL, YR, B), F32),
            pltpu.VMEM((ZL, YR, B), F32),
            pltpu.VMEM((ZL, ZH, 16, B), BF16),
            pltpu.VMEM((Z - 1, 16, B), BF16),
            dma((G, 2)),
            dma((G, 2)),
            dma,
            dma,
            dma((G + 1,)),
            dma((G + 1,)),
            dma((G,)),
            dma((G,)),
            dma((G,)),
            dma((G,)),
            dma((G,)),
            dma((G,)),
            dma,
            dma,
            pltpu.SemaphoreType.REGULAR((4,)),
        ],
        compiler_params=pltpu.CompilerParams(
            collective_id=0, has_side_effects=True, vmem_limit_bytes=64 * 1024 * 1024
        ),
        name="packed_grads",
    )(queries, keys, values, grad_out, proj_in, segments)
    x = lax.axis_index("seq") % X
    width = B // X
    return out[:8], lax.dynamic_slice(out, (8, x * width), (8, width))


def solution(mesh, gr=REAL):
    in_specs = (P("dp", "seq", None),) * 5 + (P("dp", None),)
    out_specs = (P("dp", "seq"), P("dp", "seq"))
    return jax.shard_map(
        functools.partial(on_device, gr), mesh=mesh, in_specs=in_specs, out_specs=out_specs, check_vma=False
    )
```

```python
import functools
import math

import jax
import jax.numpy as jnp
from jax import lax
from jax.experimental import pallas as pl
from jax.experimental.pallas import tpu as pltpu
from jax.sharding import PartitionSpec as P

MESH = pl.DeviceIdType.MESH
F32 = jnp.float32
BF16 = jnp.bfloat16
B = 128
NEG = -1e30


def nt(a, b):
    return lax.dot_general(a, b, (((1,), (1,)), ((), ())), preferred_element_type=F32)


def tn(a, b):
    return lax.dot_general(a, b, (((0,), (0,)), ((), ())), preferred_element_type=F32)


def nn(a, b):
    return lax.dot_general(a, b, (((1,), (0,)), ((), ())), preferred_element_type=F32)


class Grid:
    def __init__(self, ZH, Y, C, ZL, X):
        self.ZH, self.Y, self.C, self.ZL, self.X = ZH, Y, C, ZL, X
        self.Z = ZH * ZL
        self.G = ZL // 2


REAL = Grid(4, 4, 2, 8, 4)


def kernel(
    gr,
    q_hbm, k_hbm, v_hbm, do_hbm, pj_hbm, seg_hbm,
    out_ref,
    seg_ref,     q_v, do_v, kvw, pjw, pjt, bias, mo, mp, pw, dsw,
    own, csend, crecv, zq, zkv, zsrc, zr,
    ax0, ax1, ay0, ay1, by0, by1, bx0, bx1,
    ld_sem, kv_sem, pj_sem, sg_sem, hs_sem, hr_sem, cs_sem, cr_sem, ax_sem, ay_sem, by_sem, bx_sem, zs_sem, zr_sem, rel_sem,
):
    ZH, Y, ZL, X, Z, G = gr.ZH, gr.Y, gr.ZL, gr.X, gr.Z, gr.G
    HG = 2 * X
    SEQ = ZL * X
    dp, seq = lax.axis_index("dp"), lax.axis_index("seq")
    zh, y, c = dp // (2 * Y), (dp // 2) % Y, dp % 2
    zl, x = seq // X, seq % X
    z = zh * ZL + zl

    def at(zh_, y_, c_, zl_, x_):
        return ((zh_ * Y + y_) * 2 + c_, zl_ * X + x_)

    def along_z(k):
        there = lax.rem(z + k + Z, Z)
        return at(there // ZL, y, c, lax.rem(there, ZL), x)

    def along_y(k):
        return at(zh, lax.rem(y + k + Y, Y), c, zl, x)

    def along_x(k):
        return at(zh, y, c, zl, lax.rem(x + k + X, X))

    other = at(zh, y, 1 - c, zl, x)
    right = (dp, jnp.minimum(seq + 1, SEQ - 1))
    left = (dp, jnp.maximum(seq - 1, 0))

    def local(src, dst, sem):
        copy = pltpu.make_async_copy(src, dst, sem)
        copy.start()
        return copy

    def remote(src, dst, ssem, rsem, device):
        return pltpu.make_async_remote_copy(src, dst, ssem, rsem, device_id=device, device_id_type=MESH)

    def await_bytes(ref, sem):
        pltpu.make_async_copy(ref, ref, sem).wait()

    seg_in = local(seg_hbm, seg_ref, sg_sem)
    kv_in = []
    for g in range(G):
        cols = pl.ds(g * B, B)
        kv_in.append(local(k_hbm.at[0, :, cols], kvw.at[g, 0, pl.ds(0, B)], kv_sem.at[g, 0]))
        kv_in.append(local(v_hbm.at[0, :, cols], kvw.at[g, 1, pl.ds(0, B)], kv_sem.at[g, 1]))
    pj_in = local(pj_hbm.at[0], pjw.at[0], pj_sem)
    big = []
    for g in range(G):
        cols = pl.ds(g * HG * B, HG * B)
        big.append(
            (
                local(q_hbm.at[0, :, cols], q_v.at[:, cols], ld_sem.at[g, 0]),
                local(do_hbm.at[0, :, cols], do_v.at[:, cols], ld_sem.at[g, 1]),
            )
        )

    barrier = pltpu.get_barrier_semaphore()
    near = [other]
    near += [along(k) for along in (along_x, along_y, along_z) for k in (1, -1)]
    for device in near:
        pl.semaphore_signal(barrier, inc=1, device_id=device, device_id_type=MESH)

    @pl.when(seq > 0)
    def _():
        pl.semaphore_signal(barrier, inc=1, device_id=left, device_id_type=MESH)

    seg_in.wait()
    start = pl.multiple_of(seq * B, B)
    start_before = pl.multiple_of(jnp.maximum(seq - 1, 0) * B, B)
    seg_i = jnp.broadcast_to(seg_ref[:, pl.ds(start, B)].astype(F32), (B, B))
    seg_p = jnp.broadcast_to(seg_ref[:, pl.ds(start_before, B)].astype(F32), (B, B))
    seg_p = jnp.where(seq > 0, seg_p, -1.0)
    row = lax.broadcasted_iota(jnp.int32, (B, B), 0)
    lane = lax.broadcasted_iota(jnp.int32, (B, B), 1)
    causal = row <= lane
    same = jnp.where(causal, seg_i.T, seg_p.T) == seg_i
    one_bias = jnp.where(same, 0.0, NEG)
    one_mo = jnp.where(causal, 1.0, 0.0).astype(BF16)
    one_mp = jnp.where(causal, 0.0, 1.0).astype(BF16)
    for half in range(2):
        cols = pl.ds(half * B, B)
        bias[:, cols] = one_bias
        mo[:, cols] = one_mo
        mp[:, cols] = one_mp

    for copy in kv_in:
        copy.wait()
    pj_in.wait()

    @pl.when(seq < SEQ - 1)
    def _():
        pl.semaphore_wait(barrier, len(near) + 1)

    @pl.when(seq == SEQ - 1)
    def _():
        pl.semaphore_wait(barrier, len(near))

    def halo_kv(g):
        return remote(
            kvw.at[g, :, pl.ds(0, B)], kvw.at[g, :, pl.ds(B, B)], hs_sem.at[g], hr_sem.at[g], right
        )

    halo_pj = remote(pjw.at[0], pjw.at[1], hs_sem.at[G], hr_sem.at[G], right)

    @pl.when(seq < SEQ - 1)
    def _():
        halo_kv(0).start()
        halo_pj.start()
        for g in range(1, G):
            halo_kv(g).start()

    @pl.when(seq == 0)
    def _():
        kvw[:, :, B:] = jnp.zeros((G, 2, B, B), BF16)
        pjw[1] = jnp.zeros(pjw.shape[1:], BF16)

    relays = []
    reach = 1
    while reach < Z // 2:
        relays.append(reach)
        reach *= 2

    def relay_out(n):
        ways = (along_z, along_x, along_y) if n == 0 else (along_z,)
        for along in ways:
            for k in (relays[n], -relays[n]):
                pl.semaphore_signal(rel_sem.at[n], inc=1, device_id=along(k), device_id_type=MESH)

    def relay_in(n):
        pl.semaphore_wait(rel_sem.at[n], 6 if n == 0 else 2)

    relay_out(0)

    first_core = c == 0

    def transposed(n):
        t = pjw[n].astype(F32).T
        mine, theirs = [], []
        for yy in range(Y):
            for hh in range(ZH):
                o = (hh * Y + yy) * 2
                even, odd = t[o * 8 : o * 8 + 8], t[o * 8 + 8 : o * 8 + 16]
                mine.append(jnp.where(first_core, even, odd))
                theirs.append(jnp.where(first_core, odd, even))
        pjt[:, n * B : (n + 1) * B] = jnp.concatenate(mine + theirs, axis=0).astype(BF16)

    transposed(0)
    R = pjt.shape[0] // 2
    YR = R // Y

    scale = B**-0.5
    to_log2 = scale * math.log2(math.e)
    row2 = lax.broadcasted_iota(jnp.int32, (B, 2 * B), 0)
    lane2 = lax.broadcasted_iota(jnp.int32, (B, 2 * B), 1)
    causal2 = row2 <= jnp.bitwise_and(lane2, B - 1)

    def stacked(ref, off, count):
        return jnp.concatenate([ref[:, off + n * B : off + (n + 1) * B] for n in range(count)], axis=0)

    def compute(g):
        base = g * HG * B
        for copy in big[g]:
            copy.wait()
        if g == 0:
            relay_in(0)
            relay_out(1)

        @pl.when(seq > 0)
        def _():
            halo_kv(g).wait_recv()

        kw, vw = kvw[g, 0], kvw[g, 1]
        for hp in range(HG // 2):
            off = base + hp * 2 * B
            st = nt(kw, stacked(q_v, off, 2))
            dpt = nt(vw, stacked(do_v, off, 2))
            s = jnp.where(causal2, st[:B], st[B:]) * to_log2 + bias[...]
            p = jnp.exp2(s - jnp.max(s, axis=0, keepdims=True))
            p = p * (1.0 / jnp.sum(p, axis=0, keepdims=True))
            d = jnp.where(causal2, dpt[:B], dpt[B:])
            delta = jnp.sum(p * d, axis=0, keepdims=True)
            ds = (p * ((d - delta) * scale)).astype(BF16)
            pb = p.astype(BF16)
            cols = pl.ds(hp * 2 * B, 2 * B)
            pw[:B, cols] = pb * mo[...]
            pw[B:, cols] = pb * mp[...]
            dsw[:B, cols] = ds * mo[...]
            dsw[B:, cols] = ds * mp[...]
        if g == 0:

            @pl.when(seq > 0)
            def _():
                halo_pj.wait_recv()

            transposed(1)
        else:
            step0(g - 1)
        if g == 1:
            relay_in(1)
            relay_out(2)
        if g == 3:
            relay_in(2)
            relay_out(3)
        dqt = tn(kw, dsw[...]).astype(BF16)
        dk = nn(dsw[...], stacked(q_v, base, HG))
        dv = nn(pw[...], stacked(do_v, base, HG))
        for hp in range(HG // 2):
            lo = hp * 2 * B
            pair = jnp.concatenate([dqt[:, lo : lo + B], dqt[:, lo + B : lo + 2 * B]], axis=0)
            gq = nt(pjt[:, :B], pair)
            for n in range(2):
                own[g, 2 * hp + n] = gq[:R, n * B : (n + 1) * B]
                csend[g, 2 * hp + n] = gq[R:, n * B : (n + 1) * B].astype(BF16)
        gkv = nn(pjt[...], jnp.concatenate([dk, dv], axis=1).astype(BF16))
        for n in range(2):
            own[g, HG + n] = gkv[:R, n * B : (n + 1) * B]
            csend[g, HG + n] = gkv[R:, n * B : (n + 1) * B].astype(BF16)

    def core_copy(g):
        return remote(csend.at[g], crecv.at[g], cs_sem.at[g], cr_sem.at[g], other)

    class Exchange:
        def __init__(self, place, along, blocks, got, sem):
            self.place, self.along, self.blocks, self.got, self.sem = place, along, blocks, got, sem

        def start(self, g):
            for k in (2, 1, 3):
                remote(
                    self.blocks.at[g, lax.rem(self.place + k, 4)],
                    self.got.at[g, k - 1],
                    self.sem.at[g, 0],
                    self.sem.at[g, 1],
                    self.along(k),
                ).start()

        def total(self, g):
            await_bytes(self.got.at[g], self.sem.at[g, 1])
            total = self.blocks[g, self.place].astype(F32)
            for n in range(3):
                total = total + self.got[g, n].astype(F32)
            return total

        def sent(self, g):
            await_bytes(self.got.at[g], self.sem.at[g, 0])

    on_ax = Exchange(x, along_x, ax0, ax1, ax_sem)
    on_ay = Exchange(y, along_y, ay0, ay1, ay_sem)
    on_by = Exchange(y, along_y, by0, by1, by_sem)
    on_bx = Exchange(x, along_x, bx0, bx1, bx_sem)

    def step0(g):
        core_copy(g).wait_recv()
        for n in range(X):
            ax0[g, n] = (own[g, X + n] + crecv[g, X + n].astype(F32)).astype(BF16)
        on_ax.start(g)
        for at_, b in enumerate([*range(X), HG, HG + 1]):
            both = (own[g, b] + crecv[g, b].astype(F32)).astype(BF16)
            for n in range(Y):
                by0[g, n, at_ * YR : (at_ + 1) * YR] = both[n * YR : (n + 1) * YR]
        on_by.start(g)

    def step1(g):
        total = on_ax.total(g).astype(BF16)
        for n in range(Y):
            ay0[g, n] = total[n * YR : (n + 1) * YR]
        on_ay.start(g)
        total = on_by.total(g).astype(BF16)
        for n in range(X):
            bx0[g, n, :YR] = total[n * YR : (n + 1) * YR]
            bx0[g, n, YR:] = total[X * YR :]
        on_bx.start(g)

    def step2(g):
        zq[2 * g + 1] = on_ay.total(g)
        total = on_bx.total(g)
        zq[2 * g] = total[:YR]
        zkv[g] = total[YR : 2 * YR]
        zkv[G + g] = total[2 * YR :]

    built, sent = set(), set()

    def z_send(done, parts):
        ready = [n for n in range(ZL) if n // 2 < done and n % G < done]
        for n in ready:
            if n not in built:
                built.add(n)
                for hh in range(ZH):
                    rows = pl.ds(hh * 8, 8)
                    zsrc[n, hh] = jnp.concatenate([zq[n, rows], zkv[n, rows]], axis=0).astype(BF16)
        for zh_to in parts:
            for n in ready:
                if (n, zh_to) in sent:
                    continue
                sent.add((n, zh_to))
                k = lax.rem(zh_to * ZL + n - z + Z, Z)

                @pl.when(k != 0)
                def _():
                    remote(
                        zsrc.at[n, zh_to], zr.at[k - 1], zs_sem, zr_sem, at(zh_to, y, c, n, x)
                    ).start()

    for g in range(G):
        compute(g)
        core_copy(g).start()
    step1(0)
    step0(3)
    step1(1)
    step1(2)
    step2(0)
    step1(3)
    step2(1)
    relay_in(3)
    z_send(2, (0, 1, 2))
    step2(2)
    z_send(3, (0, 1))
    step2(3)
    z_send(4, (0, 1, 2, 3))

    @pl.when(seq < SEQ - 1)
    def _():
        for g in range(G):
            halo_kv(g).wait_send()
        halo_pj.wait_send()

    for g in range(G):
        core_copy(g).wait_send()
        for ring in (on_ax, on_ay, on_by, on_bx):
            ring.sent(g)
    await_bytes(zr, zs_sem)
    await_bytes(zr, zr_sem)
    total = zsrc[zl, zh].astype(F32)
    for k in range(Z - 1):
        total = total + zr[k].astype(F32)
    out_ref[...] = total


def on_device(gr, queries, keys, values, grad_out, proj_in, segments):
    G, X, Y, ZH, ZL, Z = gr.G, gr.X, gr.Y, gr.ZH, gr.ZL, gr.Z
    HG = 2 * X
    NB = HG + 2
    rank = proj_in.shape[-1]
    R = rank // 2
    YR = R // Y
    hbm = pl.BlockSpec(memory_space=pltpu.HBM)
    vmem = pl.BlockSpec(memory_space=pltpu.VMEM)
    dma = pltpu.SemaphoreType.DMA

    def exchange(rows):
        return [pltpu.VMEM((G, 4, rows, B), BF16), pltpu.VMEM((G, 3, rows, B), BF16)]

    out = pl.pallas_call(
        functools.partial(kernel, gr),
        out_shape=jax.ShapeDtypeStruct((16, B), F32),
        in_specs=[hbm] * 6,
        out_specs=vmem,
        scratch_shapes=[
            pltpu.VMEM(segments.shape, jnp.int32),
            pltpu.VMEM((B, G * HG * B), BF16),
            pltpu.VMEM((B, G * HG * B), BF16),
            pltpu.VMEM((G, 2, 2 * B, B), BF16),
            pltpu.VMEM((2, B, rank), BF16),
            pltpu.VMEM((rank, 2 * B), BF16),
            pltpu.VMEM((B, 2 * B), F32),
            pltpu.VMEM((B, 2 * B), BF16),
            pltpu.VMEM((B, 2 * B), BF16),
            pltpu.VMEM((2 * B, HG * B), BF16),
            pltpu.VMEM((2 * B, HG * B), BF16),
            pltpu.VMEM((G, NB, R, B), F32),
            pltpu.VMEM((G, NB, R, B), BF16),
            pltpu.VMEM((G, NB, R, B), BF16),
            pltpu.VMEM((ZL, YR, B), F32),
            pltpu.VMEM((ZL, YR, B), F32),
            pltpu.VMEM((ZL, ZH, 16, B), BF16),
            pltpu.VMEM((Z - 1, 16, B), BF16),
            *exchange(R),
            *exchange(YR),
            *exchange((X + 2) * YR),
            *exchange(3 * YR),
            dma((G, 2)),
            dma((G, 2)),
            dma,
            dma,
            dma((G + 1,)),
            dma((G + 1,)),
            dma((G,)),
            dma((G,)),
            dma((G, 2)),
            dma((G, 2)),
            dma((G, 2)),
            dma((G, 2)),
            dma,
            dma,
            pltpu.SemaphoreType.REGULAR((4,)),
        ],
        compiler_params=pltpu.CompilerParams(
            collective_id=0, has_side_effects=True, vmem_limit_bytes=64 * 1024 * 1024
        ),
        name="packed_grads",
    )(queries, keys, values, grad_out, proj_in, segments)
    x = lax.axis_index("seq") % X
    width = B // X
    return out[:8], lax.dynamic_slice(out, (8, x * width), (8, width))


def solution(mesh, gr=REAL):
    in_specs = (P("dp", "seq", None),) * 5 + (P("dp", None),)
    out_specs = (P("dp", "seq"), P("dp", "seq"))
    return jax.shard_map(
        functools.partial(on_device, gr), mesh=mesh, in_specs=in_specs, out_specs=out_specs, check_vma=False
    )
```

```python
import functools
import math

import jax
import jax.numpy as jnp
from jax import lax
from jax.experimental import pallas as pl
from jax.experimental.pallas import tpu as pltpu
from jax.sharding import PartitionSpec as P

MESH = pl.DeviceIdType.MESH
F32 = jnp.float32
BF16 = jnp.bfloat16
B = 128
NEG = -1e30


def nt(a, b):
    return lax.dot_general(a, b, (((1,), (1,)), ((), ())), preferred_element_type=F32)


def tn(a, b):
    return lax.dot_general(a, b, (((0,), (0,)), ((), ())), preferred_element_type=F32)


def nn(a, b):
    return lax.dot_general(a, b, (((1,), (0,)), ((), ())), preferred_element_type=F32)


class Grid:
    def __init__(self, ZH, Y, C, ZL, X):
        self.ZH, self.Y, self.C, self.ZL, self.X = ZH, Y, C, ZL, X
        self.Z = ZH * ZL
        self.G = ZL // 2


REAL = Grid(4, 4, 2, 8, 4)


def kernel(
    gr,
    q_hbm, k_hbm, v_hbm, do_hbm, pj_hbm, seg_hbm,
    out_ref,
    seg_ref,     q_v, do_v, kvw, pjw, pjt, bias, mo, mp, pw, dsw,
    own, csend, crecv, zq, zkv, zsrc, zr,
    ax0, ax1, ay0, ay1, by0, by1, bx0, bx1,
    ld_sem, kv_sem, pj_sem, sg_sem, hs_sem, hr_sem, cs_sem, cr_sem, ax_sem, ay_sem, by_sem, bx_sem, zs_sem, zr_sem, rel_sem,
):
    ZH, Y, ZL, X, Z, G = gr.ZH, gr.Y, gr.ZL, gr.X, gr.Z, gr.G
    HG = 2 * X
    SEQ = ZL * X
    dp, seq = lax.axis_index("dp"), lax.axis_index("seq")
    zh, y, c = dp // (2 * Y), (dp // 2) % Y, dp % 2
    zl, x = seq // X, seq % X
    z = zh * ZL + zl

    def at(zh_, y_, c_, zl_, x_):
        return ((zh_ * Y + y_) * 2 + c_, zl_ * X + x_)

    def along_z(k):
        there = lax.rem(z + k + Z, Z)
        return at(there // ZL, y, c, lax.rem(there, ZL), x)

    def along_y(k):
        return at(zh, lax.rem(y + k + Y, Y), c, zl, x)

    def along_x(k):
        return at(zh, y, c, zl, lax.rem(x + k + X, X))

    other = at(zh, y, 1 - c, zl, x)
    right = (dp, jnp.minimum(seq + 1, SEQ - 1))
    left = (dp, jnp.maximum(seq - 1, 0))

    def local(src, dst, sem):
        copy = pltpu.make_async_copy(src, dst, sem)
        copy.start()
        return copy

    def remote(src, dst, ssem, rsem, device):
        return pltpu.make_async_remote_copy(src, dst, ssem, rsem, device_id=device, device_id_type=MESH)

    def await_bytes(ref, sem):
        pltpu.make_async_copy(ref, ref, sem).wait()

    barrier = pltpu.get_barrier_semaphore()
    near = [other]
    near += [along(k) for along in (along_x, along_y, along_z) for k in (1, -1)]
    for device in near:
        pl.semaphore_signal(barrier, inc=1, device_id=device, device_id_type=MESH)

    @pl.when(seq > 0)
    def _():
        pl.semaphore_signal(barrier, inc=1, device_id=left, device_id_type=MESH)

    seg_in = local(seg_hbm, seg_ref, sg_sem)
    kv_in = []
    for g in range(G):
        cols = pl.ds(g * B, B)
        kv_in.append(local(k_hbm.at[0, :, cols], kvw.at[g, 0, pl.ds(0, B)], kv_sem.at[g, 0]))
        kv_in.append(local(v_hbm.at[0, :, cols], kvw.at[g, 1, pl.ds(0, B)], kv_sem.at[g, 1]))
    pj_in = local(pj_hbm.at[0], pjw.at[0], pj_sem)
    big = []
    for g in range(G):
        cols = pl.ds(g * HG * B, HG * B)
        big.append(
            (
                local(q_hbm.at[0, :, cols], q_v.at[:, cols], ld_sem.at[g, 0]),
                local(do_hbm.at[0, :, cols], do_v.at[:, cols], ld_sem.at[g, 1]),
            )
        )

    seg_in.wait()
    start = pl.multiple_of(seq * B, B)
    start_before = pl.multiple_of(jnp.maximum(seq - 1, 0) * B, B)
    seg_i = jnp.broadcast_to(seg_ref[:, pl.ds(start, B)].astype(F32), (B, B))
    seg_p = jnp.broadcast_to(seg_ref[:, pl.ds(start_before, B)].astype(F32), (B, B))
    seg_p = jnp.where(seq > 0, seg_p, -1.0)
    row = lax.broadcasted_iota(jnp.int32, (B, B), 0)
    lane = lax.broadcasted_iota(jnp.int32, (B, B), 1)
    causal = row <= lane
    same = jnp.where(causal, seg_i.T, seg_p.T) == seg_i
    one_bias = jnp.where(same, 0.0, NEG)
    one_mo = jnp.where(causal, 1.0, 0.0).astype(BF16)
    one_mp = jnp.where(causal, 0.0, 1.0).astype(BF16)
    for half in range(2):
        cols = pl.ds(half * B, B)
        bias[:, cols] = one_bias
        mo[:, cols] = one_mo
        mp[:, cols] = one_mp

    for copy in kv_in:
        copy.wait()
    pj_in.wait()

    @pl.when(seq < SEQ - 1)
    def _():
        pl.semaphore_wait(barrier, len(near) + 1)

    @pl.when(seq == SEQ - 1)
    def _():
        pl.semaphore_wait(barrier, len(near))

    def halo_kv(g):
        return remote(
            kvw.at[g, :, pl.ds(0, B)], kvw.at[g, :, pl.ds(B, B)], hs_sem.at[g], hr_sem.at[g], right
        )

    halo_pj = remote(pjw.at[0], pjw.at[1], hs_sem.at[G], hr_sem.at[G], right)

    @pl.when(seq < SEQ - 1)
    def _():
        halo_kv(0).start()
        halo_pj.start()
        for g in range(1, G):
            halo_kv(g).start()

    @pl.when(seq == 0)
    def _():
        kvw[:, :, B:] = jnp.zeros((G, 2, B, B), BF16)
        pjw[1] = jnp.zeros(pjw.shape[1:], BF16)

    relays = []
    reach = 1
    while reach < Z // 2:
        relays.append(reach)
        reach *= 2

    def relay_out(n):
        ways = (along_z, along_x, along_y) if n == 0 else (along_z,)
        for along in ways:
            for k in (relays[n], -relays[n]):
                pl.semaphore_signal(rel_sem.at[n], inc=1, device_id=along(k), device_id_type=MESH)

    def relay_in(n):
        pl.semaphore_wait(rel_sem.at[n], 6 if n == 0 else 2)

    relay_out(0)

    first_core = c == 0

    def transposed(n):
        t = pjw[n].astype(F32).T
        mine, theirs = [], []
        for yy in range(Y):
            for hh in range(ZH):
                o = (hh * Y + yy) * 2
                even, odd = t[o * 8 : o * 8 + 8], t[o * 8 + 8 : o * 8 + 16]
                mine.append(jnp.where(first_core, even, odd))
                theirs.append(jnp.where(first_core, odd, even))
        pjt[:, n * B : (n + 1) * B] = jnp.concatenate(mine + theirs, axis=0).astype(BF16)

    transposed(0)
    R = pjt.shape[0] // 2
    YR = R // Y

    scale = B**-0.5
    to_log2 = scale * math.log2(math.e)
    row2 = lax.broadcasted_iota(jnp.int32, (B, 2 * B), 0)
    lane2 = lax.broadcasted_iota(jnp.int32, (B, 2 * B), 1)
    causal2 = row2 <= jnp.bitwise_and(lane2, B - 1)

    def stacked(ref, off, count):
        return jnp.concatenate([ref[:, off + n * B : off + (n + 1) * B] for n in range(count)], axis=0)

    def compute(g):
        base = g * HG * B
        for copy in big[g]:
            copy.wait()
        if g == 0:
            relay_in(0)
            relay_out(1)

        @pl.when(seq > 0)
        def _():
            halo_kv(g).wait_recv()

        kw, vw = kvw[g, 0], kvw[g, 1]
        for hp in range(HG // 2):
            off = base + hp * 2 * B
            st = nt(kw, stacked(q_v, off, 2))
            dpt = nt(vw, stacked(do_v, off, 2))
            s = jnp.where(causal2, st[:B], st[B:]) * to_log2 + bias[...]
            p = jnp.exp2(s - jnp.max(s, axis=0, keepdims=True))
            p = p * (1.0 / jnp.sum(p, axis=0, keepdims=True))
            d = jnp.where(causal2, dpt[:B], dpt[B:])
            delta = jnp.sum(p * d, axis=0, keepdims=True)
            ds = (p * ((d - delta) * scale)).astype(BF16)
            pb = p.astype(BF16)
            cols = pl.ds(hp * 2 * B, 2 * B)
            pw[:B, cols] = pb * mo[...]
            pw[B:, cols] = pb * mp[...]
            dsw[:B, cols] = ds * mo[...]
            dsw[B:, cols] = ds * mp[...]
        if g == 0:

            @pl.when(seq > 0)
            def _():
                halo_pj.wait_recv()

            transposed(1)
        else:
            step0(g - 1)
        if g == 1:
            relay_in(1)
            relay_out(2)
        if g == 3:
            relay_in(2)
            relay_out(3)
        dqt = tn(kw, dsw[...]).astype(BF16)
        dk = nn(dsw[...], stacked(q_v, base, HG))
        dv = nn(pw[...], stacked(do_v, base, HG))
        for hp in range(HG // 2):
            lo = hp * 2 * B
            pair = jnp.concatenate([dqt[:, lo : lo + B], dqt[:, lo + B : lo + 2 * B]], axis=0)
            gq = nt(pjt[:, :B], pair)
            for n in range(2):
                own[g, 2 * hp + n] = gq[:R, n * B : (n + 1) * B]
                csend[g, 2 * hp + n] = gq[R:, n * B : (n + 1) * B].astype(BF16)
        gkv = nn(pjt[...], jnp.concatenate([dk, dv], axis=1).astype(BF16))
        for n in range(2):
            own[g, HG + n] = gkv[:R, n * B : (n + 1) * B]
            csend[g, HG + n] = gkv[R:, n * B : (n + 1) * B].astype(BF16)

    def core_copy(g):
        return remote(csend.at[g], crecv.at[g], cs_sem.at[g], cr_sem.at[g], other)

    class Exchange:
        def __init__(self, place, along, blocks, got, sem):
            self.place, self.along, self.blocks, self.got, self.sem = place, along, blocks, got, sem

        def start(self, g):
            for k in (2, 1, 3):
                remote(
                    self.blocks.at[g, lax.rem(self.place + k, 4)],
                    self.got.at[g, k - 1],
                    self.sem.at[g, 0],
                    self.sem.at[g, 1],
                    self.along(k),
                ).start()

        def total(self, g):
            await_bytes(self.got.at[g], self.sem.at[g, 1])
            total = self.blocks[g, self.place].astype(F32)
            for n in range(3):
                total = total + self.got[g, n].astype(F32)
            return total

        def sent(self, g):
            await_bytes(self.got.at[g], self.sem.at[g, 0])

    on_ax = Exchange(x, along_x, ax0, ax1, ax_sem)
    on_ay = Exchange(y, along_y, ay0, ay1, ay_sem)
    on_by = Exchange(y, along_y, by0, by1, by_sem)
    on_bx = Exchange(x, along_x, bx0, bx1, bx_sem)

    def step0(g):
        core_copy(g).wait_recv()
        for n in range(X):
            ax0[g, n] = (own[g, X + n] + crecv[g, X + n].astype(F32)).astype(BF16)
        on_ax.start(g)
        for at_, b in enumerate([*range(X), HG, HG + 1]):
            both = (own[g, b] + crecv[g, b].astype(F32)).astype(BF16)
            for n in range(Y):
                by0[g, n, at_ * YR : (at_ + 1) * YR] = both[n * YR : (n + 1) * YR]
        on_by.start(g)

    def step1(g):
        total = on_ax.total(g).astype(BF16)
        for n in range(Y):
            ay0[g, n] = total[n * YR : (n + 1) * YR]
        on_ay.start(g)
        total = on_by.total(g).astype(BF16)
        for n in range(X):
            bx0[g, n, :YR] = total[n * YR : (n + 1) * YR]
            bx0[g, n, YR:] = total[X * YR :]
        on_bx.start(g)

    def step2(g):
        zq[2 * g + 1] = on_ay.total(g)
        total = on_bx.total(g)
        zq[2 * g] = total[:YR]
        zkv[g] = total[YR : 2 * YR]
        zkv[G + g] = total[2 * YR :]

    built, sent = set(), set()

    def z_send(done, parts):
        ready = [n for n in range(ZL) if n // 2 < done and n % G < done]
        for n in ready:
            if n not in built:
                built.add(n)
                for hh in range(ZH):
                    rows = pl.ds(hh * 8, 8)
                    zsrc[n, hh] = jnp.concatenate([zq[n, rows], zkv[n, rows]], axis=0).astype(BF16)
        for zh_to in parts:
            for n in ready:
                if (n, zh_to) in sent:
                    continue
                sent.add((n, zh_to))
                k = lax.rem(zh_to * ZL + n - z + Z, Z)

                @pl.when(k != 0)
                def _():
                    remote(
                        zsrc.at[n, zh_to], zr.at[k - 1], zs_sem, zr_sem, at(zh_to, y, c, n, x)
                    ).start()

    for g in range(G):
        compute(g)
        core_copy(g).start()
    step1(0)
    step0(3)
    step1(1)
    step1(2)
    step2(0)
    step1(3)
    step2(1)
    relay_in(3)
    z_send(2, (0, 1, 2))
    step2(2)
    z_send(3, (0, 1))
    step2(3)
    z_send(4, (0, 1, 2, 3))

    @pl.when(seq < SEQ - 1)
    def _():
        for g in range(G):
            halo_kv(g).wait_send()
        halo_pj.wait_send()

    for g in range(G):
        core_copy(g).wait_send()
        for ring in (on_ax, on_ay, on_by, on_bx):
            ring.sent(g)
    await_bytes(zr, zs_sem)
    await_bytes(zr, zr_sem)
    total = zsrc[zl, zh].astype(F32)
    for k in range(Z - 1):
        total = total + zr[k].astype(F32)
    out_ref[...] = total


def split(X, total_ref, q_ref, kv_ref):
    x = lax.axis_index("seq") % X
    width = B // X
    q_ref[...] = total_ref[:8]
    kv = total_ref[8:, :width]
    for n in range(1, X):
        kv = jnp.where(x == n, total_ref[8:, n * width : (n + 1) * width], kv)
    kv_ref[...] = kv


def on_device(gr, queries, keys, values, grad_out, proj_in, segments):
    G, X, Y, ZH, ZL, Z = gr.G, gr.X, gr.Y, gr.ZH, gr.ZL, gr.Z
    HG = 2 * X
    NB = HG + 2
    rank = proj_in.shape[-1]
    R = rank // 2
    YR = R // Y
    hbm = pl.BlockSpec(memory_space=pltpu.HBM)
    vmem = pl.BlockSpec(memory_space=pltpu.VMEM)
    dma = pltpu.SemaphoreType.DMA

    def exchange(rows):
        return [pltpu.VMEM((G, 4, rows, B), BF16), pltpu.VMEM((G, 3, rows, B), BF16)]

    out = pl.pallas_call(
        functools.partial(kernel, gr),
        out_shape=jax.ShapeDtypeStruct((16, B), F32),
        in_specs=[hbm] * 6,
        out_specs=vmem,
        scratch_shapes=[
            pltpu.VMEM(segments.shape, jnp.int32),
            pltpu.VMEM((B, G * HG * B), BF16),
            pltpu.VMEM((B, G * HG * B), BF16),
            pltpu.VMEM((G, 2, 2 * B, B), BF16),
            pltpu.VMEM((2, B, rank), BF16),
            pltpu.VMEM((rank, 2 * B), BF16),
            pltpu.VMEM((B, 2 * B), F32),
            pltpu.VMEM((B, 2 * B), BF16),
            pltpu.VMEM((B, 2 * B), BF16),
            pltpu.VMEM((2 * B, HG * B), BF16),
            pltpu.VMEM((2 * B, HG * B), BF16),
            pltpu.VMEM((G, NB, R, B), F32),
            pltpu.VMEM((G, NB, R, B), BF16),
            pltpu.VMEM((G, NB, R, B), BF16),
            pltpu.VMEM((ZL, YR, B), F32),
            pltpu.VMEM((ZL, YR, B), F32),
            pltpu.VMEM((ZL, ZH, 16, B), BF16),
            pltpu.VMEM((Z - 1, 16, B), BF16),
            *exchange(R),
            *exchange(YR),
            *exchange((X + 2) * YR),
            *exchange(3 * YR),
            dma((G, 2)),
            dma((G, 2)),
            dma,
            dma,
            dma((G + 1,)),
            dma((G + 1,)),
            dma((G,)),
            dma((G,)),
            dma((G, 2)),
            dma((G, 2)),
            dma((G, 2)),
            dma((G, 2)),
            dma,
            dma,
            pltpu.SemaphoreType.REGULAR((4,)),
        ],
        compiler_params=pltpu.CompilerParams(
            collective_id=0, has_side_effects=True, vmem_limit_bytes=64 * 1024 * 1024
        ),
        name="packed_grads",
    )(queries, keys, values, grad_out, proj_in, segments)
    return pl.pallas_call(
        functools.partial(split, X),
        out_shape=(jax.ShapeDtypeStruct((8, B), F32), jax.ShapeDtypeStruct((8, B // X), F32)),
        in_specs=[vmem],
        out_specs=(vmem, vmem),
        name="split",
    )(out)


def solution(mesh, gr=REAL):
    in_specs = (P("dp", "seq", None),) * 5 + (P("dp", None),)
    out_specs = (P("dp", "seq"), P("dp", "seq"))
    return jax.shard_map(
        functools.partial(on_device, gr), mesh=mesh, in_specs=in_specs, out_specs=out_specs, check_vma=False
    )
```
